256 devices in a mesh: seq: 32 (over y, x, core), chan: 8 (over z).
Axes of the slice: x: 4, y: 4, z: 8, core: 2. Of those that a mesh axis runs over, the one named last changes fastest.
Arguments:
- q_proj: bfloat16 [32768, 8192], P('seq', 'chan'), may hold values from -6 to 6
- k_proj: bfloat16 [32768, 8192], P('seq', 'chan'), may hold values from -6 to 6
- v_proj: bfloat16 [32768, 8192], P('seq', 'chan'), may hold values from -6 to 6
- short_filter: float32 [3, 3, 8192], P(None, None, 'chan'), may hold values from -3 to 3
- decay_rate: float32 [64, 16], P('chan'), may hold values from 0 to 1, as said below
- residue: float32 [64, 16], P('chan'), may hold values from -1 to 1
Outputs:
- regrouped: bfloat16 [32, 8, 32, 32768], P('seq', None, None, 'chan')
The draws below stay inside these ranges and needn't reach their ends.
Inputs may be any that keep to these rules, and one draw needn't show every extreme that they name: `decay_rate`: positive rates.
All inputs are finite; a program needn't handle non-finite values.
Results may differ from the reference program's by a relative error of at most 0.012.
Values may be sent and summed in bfloat16 or wider, within the bound.
A program may use at most 128 MiB of HBM per device.

```python
import math
import jax
import jax.numpy as jnp
from jax import lax

D = 8192
HEADS = 64
MODES = 16
TOKENS = 32768
N_SEQ = 32
N_CHAN = 8


def modal_draw(key):
    base = jax.random.fold_in(key, 11)
    key_mode, key_weight = jax.random.split(base, 2)
    low_rate = math.log(0.2 / TOKENS)
    high_rate = 0.0
    strata = jnp.arange(MODES, dtype=jnp.float32)[None, :]
    position = (strata + jax.random.uniform(key_mode, (HEADS, MODES), jnp.float32)) / MODES
    decays = jnp.exp(low_rate + (high_rate - low_rate) * position).astype(jnp.float32)
    spread = jax.random.truncated_normal(key_weight, -2.5, 2.5, (HEADS, MODES), jnp.float32)
    weights = spread * jnp.sqrt(2.0 * decays / MODES)
    return (decays, weights)


def draw_decay_rate(key, part):
    return modal_draw(key)[0].astype(jnp.float32)


def draw_residue(key, part):
    return modal_draw(key)[1].astype(jnp.float32)


def block_scale(stream_key, shape, cuts, least, largest):
    factor_of, own = 1.0, jax.random.fold_in(stream_key, 6)
    for axis_at, shards_of in cuts:
        heights = jnp.exp(jax.random.uniform(jax.random.fold_in(own, axis_at), (shards_of,), jnp.float32, least / len(cuts), largest / len(cuts)))
        factor_of = factor_of * jnp.repeat(heights, shape[axis_at] // shards_of).reshape([-1 if axis == axis_at else 1 for axis in range(len(shape))])
    return factor_of


def centred(stream_key, dims, deviation, most, shards=(), kind=jnp.bfloat16):
    drawn = deviation * jax.random.normal(stream_key, dims, jnp.float32)
    if shards:
        drawn = drawn * block_scale(stream_key, dims, shards, -0.22, 0.18)
    return jnp.clip(drawn, -most, most).astype(kind)


def setup_inputs(seed: int = 0) -> dict:
    seeds = jax.random.split(jax.random.key(seed), 7)
    q_proj = centred(seeds[0], (TOKENS, D), 1.0, 6.0, ((0, 32), (1, 8)))
    k_proj = centred(seeds[1], (TOKENS, D), 1.0, 6.0, ((0, 32), (1, 8)))
    v_proj = centred(seeds[2], (TOKENS, D), 1.0, 6.0, ((0, 32), (1, 8)))
    short_filter = centred(seeds[3], (3, 3, D), 0.7, 3.0, ((2, 8),), jnp.float32)
    decay_rate = draw_decay_rate(jax.random.fold_in(seeds[6], 71), 0)
    residue = draw_residue(jax.random.fold_in(seeds[6], 71), 0)
    return {"q_proj": q_proj, "k_proj": k_proj, "v_proj": v_proj, "short_filter": short_filter, "decay_rate": decay_rate, "residue": residue}


def causal_short(current, rim, taps):
    extended = jnp.concatenate([rim, current], axis=0).astype(jnp.float32)
    return taps[0] * extended[2:] + taps[1] * extended[1:-1] + taps[2] * extended[:-2]


def modal_conv(gated, decays, residues, block_len, initial):
    length, head_count, channels = gated.shape
    block_count = length // block_len
    offsets = jnp.arange(block_len, dtype=jnp.float32)
    distance = offsets[:, None] - offsets[None, :]
    lagged = jnp.maximum(distance, 0.0)
    summed = jnp.sum(residues[:, None, None, :] * jnp.exp(-decays[:, None, None, :] * lagged[None, :, :, None]), axis=3)
    toeplitz = jnp.where(distance[None] >= 0.0, summed, jnp.float32(0.0))
    from_state = residues[:, None, :] * jnp.exp(-decays[:, None, :] * (offsets + 1.0)[None, :, None])
    kernel_aug = jnp.concatenate([toeplitz, from_state], axis=2)
    into_state = jnp.exp(-decays[:, :, None] * (block_len - 1.0 - offsets)[None, None, :])
    carry_decay = jnp.exp(-decays * block_len)[:, :, None]
    segments = gated.reshape(block_count, block_len, head_count, channels)

    def advance(carry_state, segment):
        values = segment.astype(jnp.float32)
        stacked = jnp.concatenate([values, carry_state.transpose(1, 0, 2)], axis=0)
        piece = jnp.einsum("htk,khc->thc", kernel_aug, stacked, precision=lax.Precision.HIGHEST)
        carry_state = carry_decay * carry_state + jnp.einsum("hrs,shc->hrc", into_state, values, precision=lax.Precision.HIGHEST)
        return carry_state, piece

    last_state, pieces = lax.scan(advance, initial, segments)
    return pieces.reshape(length, head_count, channels), last_state


def reference(q_proj, k_proj, v_proj, short_filter, decay_rate, residue):
    head_width = D // HEADS
    query_heads = q_proj.reshape(TOKENS, HEADS, head_width).transpose(1, 0, 2)
    key_heads = k_proj.reshape(TOKENS, HEADS, head_width).transpose(1, 0, 2)
    value_heads = v_proj.reshape(TOKENS, HEADS, head_width).transpose(1, 0, 2)
    taps_heads = short_filter.reshape(3, 3, HEADS, head_width).transpose(2, 0, 1, 3)

    def one_head(items):
        query, keys, values, taps, decays, weights = items
        rim = jnp.zeros((2, head_width), query.dtype)
        query_mix = causal_short(query, rim, taps[0]).astype(jnp.bfloat16)
        gated = (causal_short(keys, rim, taps[1]) * causal_short(values, rim, taps[2])).astype(jnp.bfloat16)
        initial = jnp.zeros((1, MODES, head_width), jnp.float32)
        convolved, _ = modal_conv(gated[:, None, :], decays[None], weights[None], min(128, TOKENS), initial)
        return (query_mix.astype(jnp.float32) * convolved[:, 0, :]).astype(jnp.bfloat16)

    mixed = lax.map(one_head, (query_heads, key_heads, value_heads, taps_heads, decay_rate, residue))
    mixed = mixed.transpose(0, 2, 1).reshape(D, TOKENS).reshape(N_CHAN, N_SEQ, D // (N_SEQ * N_CHAN), TOKENS)
    return mixed.transpose(1, 0, 2, 3)
```

```python
import functools

import jax
import jax.numpy as jnp
from jax import lax
from jax.experimental import pallas as pl
from jax.experimental.pallas import tpu as pltpu
from jax.sharding import PartitionSpec as P

MESH = pl.DeviceIdType.MESH
F32, BF16 = jnp.float32, jnp.bfloat16

ROWS = 1024
HEADS = 8
WIDE = 128
MODES = 16
BLOCK = 128
BLOCKS = ROWS // BLOCK
PAD = 16
NSEQ = 32
NCHAN = 8
SUB = 32
ROW = 8


def split(x):
    high = x.astype(BF16)
    return high, (x - high.astype(F32)).astype(BF16)


def matmul(a, b):
    return jnp.dot(a, b, preferred_element_type=F32)


def start_of(residue, chan):
    place = lax.rem(residue + 4 * lax.rem(chan, 2), 8)
    return 2 * lax.rem(place, 4) + place // 4


def residue_of(start, chan):
    return lax.rem(4 * lax.rem(start, 2) + start // 2 + 4 * lax.rem(chan, 2), 8)


def kernel(
    q_ref, k_ref, v_ref, taps_ref, decay_ref, residue_ref, out_ref,
    q_raw, k_raw, v_raw, rim, gated, q_mix, toeplitz, from_state, into_state,
    decays, part, local, row_in, col_in, col_out, state, mixed, middle,
    load_q, load_k, load_v, rim_send, rim_recv,
    local_send, row_recv, col_send, col_recv, state_send, state_recv,
    a_send, a_recv, b_send, b_recv,
):
    seq, chan = lax.axis_index("seq"), lax.axis_index("chan")
    yy, rr = seq // ROW, lax.rem(seq, ROW)

    barrier = pltpu.get_barrier_semaphore()

    @pl.loop(1, NSEQ)
    def _(i):
        pl.semaphore_signal(
            barrier, inc=1, device_id=(lax.rem(seq + i, NSEQ), chan), device_id_type=MESH
        )

    @pl.loop(1, NCHAN)
    def _(i):
        pl.semaphore_signal(
            barrier, inc=1, device_id=(seq, lax.rem(chan + i, NCHAN)), device_id_type=MESH
        )

    def load(ref, raw, sem, h):
        columns = pl.ds(pl.multiple_of(h * WIDE, WIDE), WIDE)
        return pltpu.make_async_copy(
            ref.at[:, columns], raw.at[h, pl.ds(PAD, ROWS), :], sem.at[h]
        )

    @pl.loop(0, HEADS)
    def _(h):
        load(k_ref, k_raw, load_k, h).start()
        load(v_ref, v_raw, load_v, h).start()

    @pl.loop(0, HEADS)
    def _(h):
        load(q_ref, q_raw, load_q, h).start()

    ones_at = lax.broadcasted_iota(jnp.int32, (MODES, MODES), 0) == lax.broadcasted_iota(
        jnp.int32, (MODES, MODES), 1
    )
    lane = lax.broadcasted_iota(jnp.int32, (MODES, BLOCK), 1)
    causal = lax.broadcasted_iota(jnp.int32, (BLOCK, BLOCK), 0) >= lax.broadcasted_iota(
        jnp.int32, (BLOCK, BLOCK), 1
    )

    def column(row):
        wide = jnp.where(ones_at, jnp.broadcast_to(row, (MODES, MODES)), 0.0)
        return jnp.broadcast_to(jnp.sum(wide, axis=1, keepdims=True), (MODES, WIDE))

    @pl.loop(0, HEADS)
    def _(h):
        rate = column(decay_ref[pl.ds(h, 1), :])
        weight = column(residue_ref[pl.ds(h, 1), :])
        decays[h] = rate
        lag = jnp.where(lane == 0, 0, BLOCK - lane).astype(F32)
        first = jnp.sum(weight * jnp.exp(-rate * lag), axis=0, keepdims=True)
        turned = pltpu.roll(
            jnp.broadcast_to(first, (BLOCK, BLOCK)), 0, 1, stride=1, stride_axis=0
        )
        high, low = split(jnp.where(causal, turned, 0.0))
        toeplitz[h, :, 0:BLOCK] = high
        toeplitz[h, :, BLOCK : 2 * BLOCK] = low
        high, low = split(weight * jnp.exp(-rate * (lane + 1).astype(F32)))
        high, low = high.astype(F32), low.astype(F32)
        rest = jnp.zeros((BLOCK - 3 * MODES, BLOCK), F32)
        from_state[h] = jnp.concatenate([high, low, high, rest], axis=0).T.astype(BF16)
        high, low = split(jnp.exp(-rate * (BLOCK - 1 - lane).astype(F32)))
        into_state[h, 0:MODES] = high
        into_state[h, MODES : 2 * MODES] = low

    pl.semaphore_wait(barrier, NSEQ - 1 + NCHAN - 1)

    after = lax.rem(seq + 1, NSEQ)
    rims = []
    for n, ref in enumerate((k_ref, v_ref, q_ref)):
        copy = pltpu.make_async_remote_copy(
            src_ref=ref.at[pl.ds(ROWS - PAD, PAD), :],
            dst_ref=rim.at[n],
            send_sem=rim_send.at[n],
            recv_sem=rim_recv.at[n],
            device_id=(after, chan),
            device_id_type=MESH,
        )
        copy.start()
        rims.append(copy)

    def short(raw, branch, h, row, count):
        columns = pl.ds(pl.multiple_of(h * WIDE, WIDE), WIDE)
        x = raw[h, pl.ds(row, count + PAD), :].astype(F32)
        y = taps_ref[branch, 0:1, columns] * x
        y = y + taps_ref[branch, 1:2, columns] * pltpu.roll(x, 1, 0)
        y = y + taps_ref[branch, 2:3, columns] * pltpu.roll(x, 2, 0)
        return y[PAD:]

    def gate(h, block):
        row = block * BLOCK
        g = (short(k_raw, 1, h, row, BLOCK) * short(v_raw, 2, h, row, BLOCK)).astype(BF16)
        gated[h, pl.ds(row, BLOCK), :] = g
        both = matmul(into_state[h], g)
        part[h, block] = both[0:MODES] + both[MODES : 2 * MODES]

    @pl.loop(0, HEADS)
    def _(h):
        load(k_ref, k_raw, load_k, h).wait()
        load(v_ref, v_raw, load_v, h).wait()
        for block in range(1, BLOCKS):
            gate(h, block)

    for copy in rims:
        copy.wait()

    def put_rim(raw, n, h):
        columns = pl.ds(pl.multiple_of(h * WIDE, WIDE), WIDE)
        rows = rim[n, :, columns]
        raw[h, 0:PAD, :] = jnp.where(seq > 0, rows, jnp.zeros_like(rows))

    @pl.loop(0, HEADS)
    def _(h):
        put_rim(k_raw, 0, h)
        put_rim(v_raw, 1, h)
        gate(h, 0)
        step = jnp.exp(decays[h] * -float(BLOCK))
        total = part[h, 0]
        for block in range(1, BLOCKS):
            total = step * total + part[h, block]
        local[h] = total

        @pl.when(h == rr)
        def _():
            row_in[rr] = total

        @pl.when(h != rr)
        def _():
            pltpu.make_async_remote_copy(
                src_ref=local.at[h],
                dst_ref=row_in.at[rr],
                send_sem=local_send,
                recv_sem=row_recv,
                device_id=(yy * ROW + h, chan),
                device_id_type=MESH,
            ).start()

    first = start_of(rr, chan)

    def query(i):
        h = lax.rem(first + i, HEADS)
        load(q_ref, q_raw, load_q, h).wait()
        put_rim(q_raw, 2, h)
        for block in range(BLOCKS):
            row = block * BLOCK
            q_mix[h, pl.ds(row, BLOCK), :] = short(q_raw, 0, h, row, BLOCK).astype(BF16)

    @pl.loop(0, 3)
    def _(i):
        query(i)

    seven = row_in.at[pl.ds(0, ROW - 1)]
    pltpu.make_async_copy(seven, seven, row_recv).wait()
    rate = decays[rr]
    shard = jnp.exp(rate * -float(ROWS))
    whole = jnp.exp(rate * -float(ROWS * ROW))
    total = row_in[0]
    for r in range(1, ROW):
        total = shard * total + row_in[r]
    col_out[...] = total
    col_in[yy] = total

    @pl.loop(1, NSEQ // ROW)
    def _(i):
        pltpu.make_async_remote_copy(
            src_ref=col_out,
            dst_ref=col_in.at[yy],
            send_sem=col_send,
            recv_sem=col_recv,
            device_id=(lax.rem(seq + ROW * i, NSEQ), chan),
            device_id_type=MESH,
        ).start()

    @pl.loop(3, 6)
    def _(i):
        query(i)

    three = col_in.at[pl.ds(0, NSEQ // ROW - 1)]
    pltpu.make_async_copy(three, three, col_recv).wait()
    before = jnp.zeros((MODES, WIDE), F32)
    for y in range(NSEQ // ROW - 1):
        before = jnp.where(y < yy, whole * before + col_in[y], before)
    for r in range(ROW):
        seven_out = local
        if r == 0:
            pltpu.make_async_copy(seven, seven, local_send).wait()
        seven_out[r] = before
        before = shard * before + row_in[r]

    @pl.loop(0, ROW)
    def _(r):
        @pl.when(r == rr)
        def _():
            state[rr] = local[r]

        @pl.when(r != rr)
        def _():
            pltpu.make_async_remote_copy(
                src_ref=local.at[r],
                dst_ref=state.at[rr],
                send_sem=state_send,
                recv_sem=state_recv,
                device_id=(yy * ROW + r, chan),
                device_id_type=MESH,
            ).start()

    @pl.loop(6, HEADS)
    def _(i):
        query(i)

    pltpu.make_async_copy(seven, seven, state_recv).wait()

    @pl.loop(0, HEADS)
    def _(i):
        h = lax.rem(first + i, HEADS)
        step = jnp.exp(decays[h] * -float(BLOCK))
        here = state[h]
        for block in range(BLOCKS):
            rows = pl.ds(block * BLOCK, BLOCK)
            g = gated[h, rows, :]
            high, low = split(here)
            rest = jnp.zeros((BLOCK - 3 * MODES, WIDE), BF16)
            stacked = jnp.concatenate([high, high, low, rest], axis=0)
            conv = matmul(toeplitz[h], jnp.concatenate([g, g], axis=0))
            conv = conv + matmul(from_state[h], stacked)
            m = q_mix[h, rows, :].astype(F32) * conv
            mixed[h, :, rows] = m.T.astype(BF16)
            if block < BLOCKS - 1:
                here = step * here + part[h, block]

        @pl.loop(0, WIDE // SUB)
        def _(n):
            sub = lax.rem(n + seq, WIDE // SUB)
            j = (WIDE // SUB) * h + sub
            source = mixed.at[h, pl.ds(pl.multiple_of(sub * SUB, SUB), SUB), :]

            @pl.when(j == seq)
            def _():
                pltpu.make_async_copy(source, middle.at[seq], a_recv.at[seq]).start()

            @pl.when(j != seq)
            def _():
                pltpu.make_async_remote_copy(
                    src_ref=source,
                    dst_ref=middle.at[seq],
                    send_sem=a_send,
                    recv_sem=a_recv.at[seq],
                    device_id=(j, chan),
                    device_id_type=MESH,
                ).start()

    @pl.loop(0, HEADS)
    def _(i):
        r = residue_of(lax.rem(seq // 4 - i + HEADS, HEADS), chan)
        parity = r // 4

        @pl.loop(0, NSEQ // ROW)
        def _(n):
            y = lax.rem(n + (chan - parity + 1) // 2, NSEQ // ROW)
            source = ROW * y + r
            plane = source // 4
            tokens = pl.multiple_of(lax.rem(source, 4) * ROWS, ROWS)
            place = out_ref.at[chan, :, pl.ds(tokens, ROWS)]
            block = middle.at[source]
            pltpu.make_async_copy(block, block, a_recv.at[source]).wait()

            @pl.when(plane == chan)
            def _():
                pltpu.make_async_copy(block, place, b_recv).start()

            @pl.when(plane != chan)
            def _():
                pltpu.make_async_remote_copy(
                    src_ref=block,
                    dst_ref=place,
                    send_sem=b_send,
                    recv_sem=b_recv,
                    device_id=(seq, plane),
                    device_id_type=MESH,
                ).start()

    three_out = col_in.at[pl.ds(0, NSEQ // ROW - 1)]
    pltpu.make_async_copy(three_out, three_out, col_send).wait()
    pltpu.make_async_copy(seven, seven, state_send).wait()
    sent = middle.at[pl.ds(0, NSEQ - 1)]
    pltpu.make_async_copy(sent, sent, a_send).wait()
    sent = middle.at[pl.ds(0, NSEQ - NSEQ // NCHAN)]
    pltpu.make_async_copy(sent, sent, b_send).wait()
    pltpu.make_async_copy(out_ref, out_ref, b_recv).wait()


def per_device(q_proj, k_proj, v_proj, short_filter, decay_rate, residue):
    dma = pltpu.SemaphoreType.DMA
    out = pl.pallas_call(
        kernel,
        out_shape=jax.ShapeDtypeStruct((NCHAN, SUB, 4 * ROWS), BF16),
        in_specs=[pl.BlockSpec(memory_space=pl.ANY)] * 3
        + [pl.BlockSpec(memory_space=pltpu.VMEM)] * 3,
        out_specs=pl.BlockSpec(memory_space=pl.ANY),
        scratch_shapes=[
            pltpu.VMEM((HEADS, PAD + ROWS, WIDE), BF16),
            pltpu.VMEM((HEADS, PAD + ROWS, WIDE), BF16),
            pltpu.VMEM((HEADS, PAD + ROWS, WIDE), BF16),
            pltpu.VMEM((3, PAD, HEADS * WIDE), BF16),
            pltpu.VMEM((HEADS, ROWS, WIDE), BF16),
            pltpu.VMEM((HEADS, ROWS, WIDE), BF16),
            pltpu.VMEM((HEADS, BLOCK, 2 * BLOCK), BF16),
            pltpu.VMEM((HEADS, BLOCK, BLOCK), BF16),
            pltpu.VMEM((HEADS, 2 * MODES, BLOCK), BF16),
            pltpu.VMEM((HEADS, MODES, WIDE), F32),
            pltpu.VMEM((HEADS, BLOCKS, MODES, WIDE), F32),
            pltpu.VMEM((HEADS, MODES, WIDE), F32),
            pltpu.VMEM((ROW, MODES, WIDE), F32),
            pltpu.VMEM((NSEQ // ROW, MODES, WIDE), F32),
            pltpu.VMEM((MODES, WIDE), F32),
            pltpu.VMEM((HEADS, MODES, WIDE), F32),
            pltpu.VMEM((HEADS, WIDE, ROWS), BF16),
            pltpu.VMEM((NSEQ, SUB, ROWS), BF16),
            dma((HEADS,)), dma((HEADS,)), dma((HEADS,)),
            dma((3,)), dma((3,)),
            dma, dma, dma, dma, dma, dma,
            dma, dma((NSEQ,)), dma, dma,
        ],
        compiler_params=pltpu.CompilerParams(
            collective_id=0, has_side_effects=True, vmem_limit_bytes=56 << 20
        ),
        name="hyena",
    )(q_proj, k_proj, v_proj, short_filter, decay_rate, residue)
    return out[None]


def solution(mesh):
    in_specs = (
        P("seq", "chan"),
        P("seq", "chan"),
        P("seq", "chan"),
        P(None, None, "chan"),
        P("chan", None),
        P("chan", None),
    )
    out_specs = P("seq", None, None, "chan")
    return jax.shard_map(
        per_device, mesh=mesh, in_specs=in_specs, out_specs=out_specs, check_vma=False
    )
```

```python
import functools

import jax
import jax.numpy as jnp
from jax import lax
from jax.experimental import pallas as pl
from jax.experimental.pallas import tpu as pltpu
from jax.sharding import PartitionSpec as P

MESH = pl.DeviceIdType.MESH
F32, BF16 = jnp.float32, jnp.bfloat16

ROWS = 1024
HEADS = 8
WIDE = 128
MODES = 16
BLOCK = 128
BLOCKS = ROWS // BLOCK
PAD = 16
NSEQ = 32
NCHAN = 8
SUB = 32
ROW = 8
LOADS = 4
QUERIES = 5
AHEAD = 5


def split(x):
    high = x.astype(BF16)
    return high, (x - high.astype(F32)).astype(BF16)


def matmul(a, b):
    return jnp.dot(a, b, preferred_element_type=F32)


def mod(a, b):
    return lax.rem(a, b)


def kernel(
    q_ref, k_ref, v_ref, taps_in, decay_in, residue_in, out_ref,
    taps_ref, decay_ref, residue_ref,
    q_raw, k_raw, v_raw, gated, q_mix, toeplitz, from_state, into_state,
    decays, part, local, row_in, col_in, col_out, state_out, state, mixed, middle,
    load_q, load_k, load_v, load_p, rim_send, rim_recv,
    local_send, row_recv, col_send, col_recv, state_send, state_recv,
    a_send, a_recv, b_send, b_recv,
):
    seq, chan = lax.axis_index("seq"), lax.axis_index("chan")
    yy, rr = seq // ROW, mod(seq, ROW)

    def columns_of(h):
        return pl.ds(pl.multiple_of(h * WIDE, WIDE), WIDE)

    def load(ref, raw, sem, n, parts):
        width = HEADS * WIDE // parts
        columns = pl.ds(pl.multiple_of(n * width, width), width)
        return pltpu.make_async_copy(
            ref.at[:, columns], raw.at[pl.ds(PAD, ROWS), columns], sem.at[n]
        )

    barrier = pltpu.get_barrier_semaphore()

    def here_for(to_seq, to_chan):
        pl.semaphore_signal(barrier, inc=1, device_id=(to_seq, to_chan), device_id_type=MESH)

    for i in range(1, ROW):
        here_for(yy * ROW + mod(rr + i, ROW), chan)

    @pl.when(jnp.logical_and(rr == 0, yy > 0))
    def _():
        here_for(seq - 1, chan)

    for i in range(1, NSEQ // ROW):
        here_for(mod(seq + i * ROW, NSEQ), chan)

    params = [
        pltpu.make_async_copy(a, b, load_p.at[n])
        for n, (a, b) in enumerate(
            ((taps_in, taps_ref), (decay_in, decay_ref), (residue_in, residue_ref))
        )
    ]
    for copy in params:
        copy.start()
    for n in range(LOADS):
        load(k_ref, k_raw, load_k, n, LOADS).start()
        load(v_ref, v_raw, load_v, n, LOADS).start()
    load(q_ref, q_raw, load_q, 0, 1).start()
    for i in range(1, NCHAN):
        here_for(seq, mod(chan + i, NCHAN))
    for copy in params:
        copy.wait()

    ones_at = lax.broadcasted_iota(jnp.int32, (MODES, MODES), 0) == lax.broadcasted_iota(
        jnp.int32, (MODES, MODES), 1
    )
    lane = lax.broadcasted_iota(jnp.int32, (MODES, BLOCK), 1)
    causal = lax.broadcasted_iota(jnp.int32, (BLOCK, BLOCK), 0) >= lax.broadcasted_iota(
        jnp.int32, (BLOCK, BLOCK), 1
    )

    def column(row):
        wide = jnp.where(ones_at, jnp.broadcast_to(row, (MODES, MODES)), 0.0)
        return jnp.broadcast_to(jnp.sum(wide, axis=1, keepdims=True), (MODES, WIDE))

    for h in range(HEADS):
        rate = column(decay_ref[h : h + 1, :])
        decays[h] = rate
        high, low = split(jnp.exp(-rate * (BLOCK - 1 - lane).astype(F32)))
        into_state[h, 0:MODES] = high
        into_state[h, MODES : 2 * MODES] = low

    def filters(h):
        rate = decays[h]
        weight = column(residue_ref[pl.ds(h, 1), :])
        lag = jnp.where(lane == 0, 0, BLOCK - lane).astype(F32)
        first = jnp.sum(weight * jnp.exp(-rate * lag), axis=0, keepdims=True)
        turned = pltpu.roll(
            jnp.broadcast_to(first, (BLOCK, BLOCK)), 0, 1, stride=1, stride_axis=0
        )
        high, low = split(jnp.where(causal, turned, 0.0))
        toeplitz[h, :, 0:BLOCK] = high
        toeplitz[h, :, BLOCK : 2 * BLOCK] = low
        high, low = split(weight * jnp.exp(-rate * (lane + 1).astype(F32)))
        high, low = high.astype(F32), low.astype(F32)
        rest = jnp.zeros((BLOCK - 3 * MODES, BLOCK), F32)
        from_state[h] = jnp.concatenate([high, low, high, rest], axis=0).T.astype(BF16)

    def taps_of(raw, branch, h, start, count):
        columns = columns_of(h)
        x = raw[pl.ds(start, count), columns].astype(F32)
        y = taps_ref[branch, 0:1, columns] * x
        y = y + taps_ref[branch, 1:2, columns] * pltpu.roll(x, 1, 0)
        return y + taps_ref[branch, 2:3, columns] * pltpu.roll(x, 2, 0)

    def short(raw, branch, h, row, count):
        return taps_of(raw, branch, h, row, count + PAD)[PAD:]

    inner = lax.broadcasted_iota(jnp.int32, (BLOCK, WIDE), 0) >= 2

    def gate(h, block):
        row = block * BLOCK
        if block:
            g = short(k_raw, 1, h, row, BLOCK) * short(v_raw, 2, h, row, BLOCK)
        else:
            g = taps_of(k_raw, 1, h, PAD, BLOCK) * taps_of(v_raw, 2, h, PAD, BLOCK)
            g = jnp.where(inner, g, 0.0)
        g = g.astype(BF16)
        gated[h, pl.ds(row, BLOCK), :] = g
        both = matmul(into_state[h], g)
        both = both[0:MODES] + both[MODES : 2 * MODES]
        part[h, block] = both
        return both

    def gates(n):
        load(k_ref, k_raw, load_k, n, LOADS).wait()
        load(v_ref, v_raw, load_v, n, LOADS).wait()
        for k in range(HEADS // LOADS):
            h = n * (HEADS // LOADS) + k
            step = jnp.exp(decays[h] * -float(BLOCK))
            total = gate(h, 0)
            for block in range(1, BLOCKS):
                total = step * total + gate(h, block)
            local[h] = total

    @pl.loop(0, LOADS // 2)
    def _(n):
        gates(n)

    ends_row = jnp.logical_and(rr == ROW - 1, yy < NSEQ // ROW - 1)
    greeted = ROW - 1 + NSEQ // ROW - 1 + NCHAN - 1

    @pl.when(ends_row)
    def _():
        pl.semaphore_wait(barrier, greeted + 1)

    @pl.when(jnp.logical_not(ends_row))
    def _():
        pl.semaphore_wait(barrier, greeted)

    def rim(n):
        ref, raw = ((k_ref, k_raw), (v_ref, v_raw), (q_ref, q_raw))[n]
        return pltpu.make_async_remote_copy(
            src_ref=ref.at[pl.ds(ROWS - PAD, PAD), :],
            dst_ref=raw.at[pl.ds(0, PAD), :],
            send_sem=rim_send.at[n],
            recv_sem=rim_recv.at[n],
            device_id=(mod(seq + 1, NSEQ), chan),
            device_id_type=MESH,
        )

    @pl.when(seq < NSEQ - 1)
    def _():
        for n in range(3):
            rim(n).start()

    @pl.when(seq == 0)
    def _():
        for raw in (k_raw, v_raw, q_raw):
            raw[0:PAD, :] = jnp.zeros((PAD, HEADS * WIDE), BF16)

    @pl.loop(LOADS // 2, LOADS)
    def _(n):
        gates(n)

    @pl.when(seq > 0)
    def _():
        for n in range(2):
            rim(n).wait_recv()

    firsts = []
    for h in range(HEADS):
        g = taps_of(k_raw, 1, h, 0, 2 * PAD) * taps_of(v_raw, 2, h, 0, 2 * PAD)
        g = g[PAD:].astype(BF16)
        gated[h, 0:PAD, :] = g
        g = g.astype(F32)[0:2]
        firsts.append(g)
        rate = decays[h]
        local[h] = (
            local[h]
            + jnp.exp(rate * -float(ROWS - 1)) * g[0:1]
            + jnp.exp(rate * -float(ROWS - 2)) * g[1:2]
        )
    row_in[rr] = local[rr]

    for i in range(1, ROW):
        h = mod(rr + i, ROW)
        pltpu.make_async_remote_copy(
            src_ref=local.at[h],
            dst_ref=row_in.at[rr],
            send_sem=local_send,
            recv_sem=row_recv,
            device_id=(yy * ROW + h, chan),
            device_id_type=MESH,
        ).start()

    for h in range(HEADS):
        g, rate = firsts[h], decays[h]
        part[h, 0] = (
            part[h, 0]
            + jnp.exp(rate * -float(BLOCK - 1)) * g[0:1]
            + jnp.exp(rate * -float(BLOCK - 2)) * g[1:2]
        )

    @pl.loop(0, HEADS)
    def _(h):
        filters(h)

    load(q_ref, q_raw, load_q, 0, 1).wait()

    @pl.when(seq > 0)
    def _():
        rim(2).wait_recv()

    side, core, half = mod(rr // 2, 2), mod(rr, 2), rr // 4
    parity = mod(half + chan, 2)
    base = 2 * (side + 2 * core) + parity + 2 * yy - 2 * ((chan + parity) // 2) + 2 * NCHAN

    def group_of(i):
        return mod(base + i, HEADS)

    def source_of(i, a, b):
        odd = mod(seq // 4 - i + HEADS, 2)
        turn = mod(seq // 4 - i - odd + HEADS, HEADS) // 2
        s, c = mod(side + a, 2), mod(core + b, 2)
        y = mod(turn - s - 2 * c + (chan + odd) // 2 + NSEQ // ROW, NSEQ // ROW)
        return ROW * y + 4 * mod(odd + chan, 2) + 2 * s + c

    def query(i):
        h = group_of(i)
        for block in range(BLOCKS):
            row = block * BLOCK
            q_mix[h, pl.ds(row, BLOCK), :] = short(q_raw, 0, h, row, BLOCK).astype(BF16)

    seven = row_in.at[pl.ds(0, ROW - 1)]
    three = col_in.at[pl.ds(0, NSEQ // ROW - 1)]
    pltpu.make_async_copy(seven, seven, row_recv).wait()
    rate = decays[rr]
    shard = jnp.exp(rate * -float(ROWS))
    whole = jnp.exp(rate * -float(ROWS * ROW))
    total = row_in[0]
    for r in range(1, ROW):
        total = shard * total + row_in[r]
    col_out[...] = total
    col_in[yy] = total

    for i in range(1, NSEQ // ROW):
        pltpu.make_async_remote_copy(
            src_ref=col_out,
            dst_ref=col_in.at[yy],
            send_sem=col_send,
            recv_sem=col_recv,
            device_id=(mod(seq + ROW * i, NSEQ), chan),
            device_id_type=MESH,
        ).start()

    @pl.loop(0, QUERIES)
    def _(i):
        query(i)

    pltpu.make_async_copy(three, three, col_recv).wait()
    before = jnp.zeros((MODES, WIDE), F32)
    for y in range(NSEQ // ROW - 1):
        before = jnp.where(y < yy, whole * before + col_in[y], before)
    for r in range(ROW):
        state_out[r] = before
        before = shard * before + row_in[r]
    state[rr] = state_out[rr]

    for i in range(1, ROW):
        r = mod(rr + i, ROW)
        pltpu.make_async_remote_copy(
            src_ref=state_out.at[r],
            dst_ref=state.at[rr],
            send_sem=state_send,
            recv_sem=state_recv,
            device_id=(yy * ROW + r, chan),
            device_id_type=MESH,
        ).start()

    @pl.loop(QUERIES, HEADS)
    def _(i):
        query(i)

    pltpu.make_async_copy(seven, seven, state_recv).wait()

    def mix(i):
        h = group_of(i)
        step = jnp.exp(decays[h] * -float(BLOCK))
        here = state[h]
        for block in range(BLOCKS):
            rows = pl.ds(block * BLOCK, BLOCK)
            g = gated[h, rows, :]
            high, low = split(here)
            rest = jnp.zeros((BLOCK - 3 * MODES, WIDE), BF16)
            stacked = jnp.concatenate([high, high, low, rest], axis=0)
            conv = matmul(toeplitz[h], jnp.concatenate([g, g], axis=0))
            conv = conv + matmul(from_state[h], stacked)
            m = q_mix[h, rows, :].astype(F32) * conv
            mixed[h, :, rows] = m.T.astype(BF16)
            if block < BLOCKS - 1:
                here = step * here + part[h, block]

    def send(i, a, b):
        h = group_of(i)
        sub = 2 * mod(side + a, 2) + mod(core + b, 2)
        j = (WIDE // SUB) * h + sub
        source = mixed.at[h, pl.ds(pl.multiple_of(sub * SUB, SUB), SUB), :]

        @pl.when(j == seq)
        def _():
            pltpu.make_async_copy(source, middle.at[seq], a_recv.at[seq]).start()

        @pl.when(j != seq)
        def _():
            pltpu.make_async_remote_copy(
                src_ref=source,
                dst_ref=middle.at[seq],
                send_sem=a_send,
                recv_sem=a_recv.at[seq],
                device_id=(j, chan),
                device_id_type=MESH,
            ).start()

    def forward(i, a, b):
        source = source_of(i, a, b)
        plane = source // 4
        tokens = pl.multiple_of(mod(source, 4) * ROWS, ROWS)
        place = out_ref.at[chan, :, pl.ds(tokens, ROWS)]
        block = middle.at[source]
        pltpu.make_async_copy(block, block, a_recv.at[source]).wait()

        @pl.when(plane == chan)
        def _():
            pltpu.make_async_copy(block, place, b_recv).start()

        @pl.when(plane != chan)
        def _():
            pltpu.make_async_remote_copy(
                src_ref=block,
                dst_ref=place,
                send_sem=b_send,
                recv_sem=b_recv,
                device_id=(seq, plane),
                device_id_type=MESH,
            ).start()

    def in_order(turn, m):
        turn(m // 4, mod(m // 2, 2), mod(m, 2))

    @pl.loop(0, NSEQ + AHEAD)
    def _(m):
        @pl.when(jnp.logical_and(m < NSEQ, mod(m, 4) == 0))
        def _():
            mix(m // 4)

        @pl.when(m < NSEQ)
        def _():
            in_order(send, m)

        @pl.when(m >= AHEAD)
        def _():
            in_order(forward, m - AHEAD)

    @pl.when(seq < NSEQ - 1)
    def _():
        for n in range(3):
            rim(n).wait_send()

    pltpu.make_async_copy(seven, seven, local_send).wait()
    pltpu.make_async_copy(three, three, col_send).wait()
    pltpu.make_async_copy(seven, seven, state_send).wait()
    sent = middle.at[pl.ds(0, NSEQ - 1)]
    pltpu.make_async_copy(sent, sent, a_send).wait()
    sent = middle.at[pl.ds(0, NSEQ - NSEQ // NCHAN)]
    pltpu.make_async_copy(sent, sent, b_send).wait()
    pltpu.make_async_copy(out_ref, out_ref, b_recv).wait()


def per_device(q_proj, k_proj, v_proj, short_filter, decay_rate, residue):
    dma = pltpu.SemaphoreType.DMA
    raw = pltpu.VMEM((PAD + ROWS, HEADS * WIDE), BF16)
    out = pl.pallas_call(
        kernel,
        out_shape=jax.ShapeDtypeStruct((NCHAN, SUB, 4 * ROWS), BF16),
        in_specs=[pl.BlockSpec(memory_space=pl.ANY)] * 6,
        out_specs=pl.BlockSpec(memory_space=pl.ANY),
        scratch_shapes=[
            pltpu.VMEM(short_filter.shape, F32),
            pltpu.VMEM(decay_rate.shape, F32),
            pltpu.VMEM(residue.shape, F32),
            raw, raw, raw,
            pltpu.VMEM((HEADS, ROWS, WIDE), BF16),
            pltpu.VMEM((HEADS, ROWS, WIDE), BF16),
            pltpu.VMEM((HEADS, BLOCK, 2 * BLOCK), BF16),
            pltpu.VMEM((HEADS, BLOCK, BLOCK), BF16),
            pltpu.VMEM((HEADS, 2 * MODES, BLOCK), BF16),
            pltpu.VMEM((HEADS, MODES, WIDE), F32),
            pltpu.VMEM((HEADS, BLOCKS, MODES, WIDE), F32),
            pltpu.VMEM((HEADS, MODES, WIDE), F32),
            pltpu.VMEM((ROW, MODES, WIDE), F32),
            pltpu.VMEM((NSEQ // ROW, MODES, WIDE), F32),
            pltpu.VMEM((MODES, WIDE), F32),
            pltpu.VMEM((ROW, MODES, WIDE), F32),
            pltpu.VMEM((HEADS, MODES, WIDE), F32),
            pltpu.VMEM((HEADS, WIDE, ROWS), BF16),
            pltpu.VMEM((NSEQ, SUB, ROWS), BF16),
            dma((1,)), dma((LOADS,)), dma((LOADS,)), dma((3,)),
            dma((3,)), dma((3,)),
            dma, dma, dma, dma, dma, dma,
            dma, dma((NSEQ,)), dma, dma,
        ],
        compiler_params=pltpu.CompilerParams(
            collective_id=0, has_side_effects=True, vmem_limit_bytes=56 << 20
        ),
        name="hyena",
    )(q_proj, k_proj, v_proj, short_filter, decay_rate, residue)
    return out[None]


def solution(mesh):
    in_specs = (
        P("seq", "chan"),
        P("seq", "chan"),
        P("seq", "chan"),
        P(None, None, "chan"),
        P("chan", None),
        P("chan", None),
    )
    out_specs = P("seq", None, None, "chan")
    return jax.shard_map(
        per_device, mesh=mesh, in_specs=in_specs, out_specs=out_specs, check_vma=False
    )
```

```python
import functools

import jax
import jax.numpy as jnp
from jax import lax
from jax.experimental import pallas as pl
from jax.experimental.pallas import tpu as pltpu
from jax.sharding import PartitionSpec as P

MESH = pl.DeviceIdType.MESH
F32, BF16 = jnp.float32, jnp.bfloat16

ROWS = 1024
HEADS = 8
WIDE = 128
MODES = 16
BLOCK = 128
BLOCKS = ROWS // BLOCK
PAD = 16
NSEQ = 32
NCHAN = 8
SUB = 32
ROW = 8
LOADS = 4
FILTERS = 1
QUERIES = 2
MORE = 5
AHEAD = 5


def split(x):
    high = x.astype(BF16)
    return high, (x - high.astype(F32)).astype(BF16)


def matmul(a, b):
    return jnp.dot(a, b, preferred_element_type=F32)


def mod(a, b):
    return lax.rem(a, b)


def kernel(
    q_ref, k_ref, v_ref, params_ref, out_ref,
    q_raw, k_raw, v_raw, gated, q_mix, toeplitz, from_state, into_state,
    decays, first_on, part, local, row_in, col_in, col_out, state_out, state, mixed, middle,
    load_q, load_k, load_v, rim_send, rim_recv,
    local_send, row_recv, col_send, col_recv, state_send, state_recv,
    a_send, a_recv, b_send, b_recv,
):
    seq, chan = lax.axis_index("seq"), lax.axis_index("chan")
    yy, rr = seq // ROW, mod(seq, ROW)

    def columns_of(h):
        return pl.ds(pl.multiple_of(h * WIDE, WIDE), WIDE)

    def load(ref, raw, sem, n, parts):
        width = HEADS * WIDE // parts
        columns = pl.ds(pl.multiple_of(n * width, width), width)
        return pltpu.make_async_copy(
            ref.at[:, columns], raw.at[pl.ds(PAD, ROWS), columns], sem.at[n]
        )

    load(k_ref, k_raw, load_k, 0, LOADS).start()
    load(v_ref, v_raw, load_v, 0, LOADS).start()

    barrier = pltpu.get_barrier_semaphore()

    def here_for(to_seq, to_chan):
        pl.semaphore_signal(barrier, inc=1, device_id=(to_seq, to_chan), device_id_type=MESH)

    for i in range(1, NCHAN):
        here_for(seq, mod(chan + i, NCHAN))
    for i in range(1, ROW):
        here_for(yy * ROW + mod(rr + i, ROW), chan)

    @pl.when(jnp.logical_and(rr == 0, yy > 0))
    def _():
        here_for(seq - 1, chan)

    for i in range(1, NSEQ // ROW):
        here_for(mod(seq + i * ROW, NSEQ), chan)

    for n in range(1, LOADS):
        load(k_ref, k_raw, load_k, n, LOADS).start()
        load(v_ref, v_raw, load_v, n, LOADS).start()
    load(q_ref, q_raw, load_q, 0, 1).start()

    ones_at = lax.broadcasted_iota(jnp.int32, (MODES, MODES), 0) == lax.broadcasted_iota(
        jnp.int32, (MODES, MODES), 1
    )
    lane = lax.broadcasted_iota(jnp.int32, (MODES, BLOCK), 1)
    causal = lax.broadcasted_iota(jnp.int32, (BLOCK, BLOCK), 0) >= lax.broadcasted_iota(
        jnp.int32, (BLOCK, BLOCK), 1
    )

    def column(row):
        wide = jnp.where(ones_at, jnp.broadcast_to(row, (MODES, MODES)), 0.0)
        return jnp.broadcast_to(jnp.sum(wide, axis=1, keepdims=True), (MODES, WIDE))

    for h in range(HEADS):
        rate = column(params_ref[3, h : h + 1, 0:MODES])
        decays[h] = rate
        first_on[h, 0] = jnp.exp(rate * -float(ROWS - 1))
        first_on[h, 1] = jnp.exp(rate * -float(ROWS - 2))
        high, low = split(jnp.exp(-rate * (BLOCK - 1 - lane).astype(F32)))
        into_state[h, 0:MODES] = high
        into_state[h, MODES : 2 * MODES] = low

    def filters(h):
        rate = decays[h]
        weight = column(params_ref[4, h : h + 1, 0:MODES])
        lag = jnp.where(lane == 0, 0, BLOCK - lane).astype(F32)
        first = jnp.sum(weight * jnp.exp(-rate * lag), axis=0, keepdims=True)
        turned = pltpu.roll(
            jnp.broadcast_to(first, (BLOCK, BLOCK)), 0, 1, stride=1, stride_axis=0
        )
        high, low = split(jnp.where(causal, turned, 0.0))
        toeplitz[h, :, 0:BLOCK] = high
        toeplitz[h, :, BLOCK : 2 * BLOCK] = low
        high, low = split(weight * jnp.exp(-rate * (lane + 1).astype(F32)))
        high, low = high.astype(F32), low.astype(F32)
        rest = jnp.zeros((BLOCK - 3 * MODES, BLOCK), F32)
        from_state[h] = jnp.concatenate([high, low, high, rest], axis=0).T.astype(BF16)

    def taps_of(raw, branch, h, start, count):
        columns = columns_of(h)
        x = raw[pl.ds(start, count), columns].astype(F32)
        y = params_ref[branch, 0:1, columns] * x
        y = y + params_ref[branch, 1:2, columns] * pltpu.roll(x, 1, 0)
        return y + params_ref[branch, 2:3, columns] * pltpu.roll(x, 2, 0)

    def short(raw, branch, h, row, count):
        return taps_of(raw, branch, h, row, count + PAD)[PAD:]

    inner = lax.broadcasted_iota(jnp.int32, (BLOCK, WIDE), 0) >= 2

    def gate(h, block):
        row = block * BLOCK
        if block:
            g = short(k_raw, 1, h, row, BLOCK) * short(v_raw, 2, h, row, BLOCK)
        else:
            g = taps_of(k_raw, 1, h, PAD, BLOCK) * taps_of(v_raw, 2, h, PAD, BLOCK)
            g = jnp.where(inner, g, 0.0)
        g = g.astype(BF16)
        gated[h, pl.ds(row, BLOCK), :] = g
        both = matmul(into_state[h], g)
        both = both[0:MODES] + both[MODES : 2 * MODES]
        part[h, block] = both
        return both

    def loaded(n):
        load(k_ref, k_raw, load_k, n, LOADS).wait()
        load(v_ref, v_raw, load_v, n, LOADS).wait()

    def gates(n):
        for k in range(HEADS // LOADS):
            h = n * (HEADS // LOADS) + k
            step = jnp.exp(decays[h] * -float(BLOCK))
            total = gate(h, 0)
            for block in range(1, BLOCKS):
                total = step * total + gate(h, block)
            local[h] = total

    loaded(0)
    gates(0)
    for n in range(1, LOADS):
        loaded(n)

    ends_row = jnp.logical_and(rr == ROW - 1, yy < NSEQ // ROW - 1)
    greeted = ROW - 1 + NSEQ // ROW - 1 + NCHAN - 1

    @pl.when(ends_row)
    def _():
        pl.semaphore_wait(barrier, greeted + 1)

    @pl.when(jnp.logical_not(ends_row))
    def _():
        pl.semaphore_wait(barrier, greeted)

    def rim(n):
        raw = (k_raw, v_raw, q_raw)[n]
        return pltpu.make_async_remote_copy(
            src_ref=raw.at[pl.ds(ROWS, PAD), :],
            dst_ref=raw.at[pl.ds(0, PAD), :],
            send_sem=rim_send.at[n],
            recv_sem=rim_recv.at[n],
            device_id=(mod(seq + 1, NSEQ), chan),
            device_id_type=MESH,
        )

    @pl.when(seq < NSEQ - 1)
    def _():
        for n in range(2):
            rim(n).start()

    @pl.when(seq == 0)
    def _():
        for raw in (k_raw, v_raw, q_raw):
            raw[0:PAD, :] = jnp.zeros((PAD, HEADS * WIDE), BF16)

    @pl.loop(1, LOADS)
    def _(n):
        gates(n)

    @pl.when(seq > 0)
    def _():
        for n in range(2):
            rim(n).wait_recv()

    firsts = []
    for h in range(HEADS):
        g = taps_of(k_raw, 1, h, 0, 2 * PAD) * taps_of(v_raw, 2, h, 0, 2 * PAD)
        g = g[PAD:].astype(BF16)
        gated[h, 0:PAD, :] = g
        g = g.astype(F32)[0:2]
        firsts.append(g)
        local[h] = local[h] + first_on[h, 0] * g[0:1] + first_on[h, 1] * g[1:2]
    row_in[rr] = local[rr]

    for i in range(1, ROW):
        h = mod(rr + i, ROW)
        pltpu.make_async_remote_copy(
            src_ref=local.at[h],
            dst_ref=row_in.at[rr],
            send_sem=local_send,
            recv_sem=row_recv,
            device_id=(yy * ROW + h, chan),
            device_id_type=MESH,
        ).start()

    load(q_ref, q_raw, load_q, 0, 1).wait()

    @pl.when(seq < NSEQ - 1)
    def _():
        rim(2).start()

    for h in range(HEADS):
        g, rate = firsts[h], decays[h]
        part[h, 0] = (
            part[h, 0]
            + jnp.exp(rate * -float(BLOCK - 1)) * g[0:1]
            + jnp.exp(rate * -float(BLOCK - 2)) * g[1:2]
        )

    side, core, half = mod(rr // 2, 2), mod(rr, 2), rr // 4
    parity = mod(half + chan, 2)
    base = 2 * (1 - side + 2 * core) + parity + 2 * yy - 2 * ((chan + parity) // 2) + 2 * NCHAN

    def group_of(i):
        return mod(base + i, HEADS)

    def source_of(i, a, b):
        odd = mod(seq // 4 - i + HEADS, 2)
        turn = mod(seq // 4 - i - odd + HEADS, HEADS) // 2
        s, c = mod(side + a, 2), mod(core + b, 2)
        y = mod(turn - (1 - s) - 2 * c + (chan + odd) // 2 + NSEQ // ROW, NSEQ // ROW)
        return ROW * y + 4 * mod(odd + chan, 2) + 2 * s + c

    def query(i):
        h = group_of(i)
        for block in range(BLOCKS):
            row = block * BLOCK
            q_mix[h, pl.ds(row, BLOCK), :] = short(q_raw, 0, h, row, BLOCK).astype(BF16)

    for h in range(FILTERS):
        filters(h)

    seven = row_in.at[pl.ds(0, ROW - 1)]
    three = col_in.at[pl.ds(0, NSEQ // ROW - 1)]
    pltpu.make_async_copy(seven, seven, row_recv).wait()
    rate = decays[rr]
    shard = jnp.exp(rate * -float(ROWS))
    whole = jnp.exp(rate * -float(ROWS * ROW))
    total = row_in[0]
    for r in range(1, ROW):
        total = shard * total + row_in[r]
    col_out[...] = total
    col_in[yy] = total

    for i in range(1, NSEQ // ROW):
        pltpu.make_async_remote_copy(
            src_ref=col_out,
            dst_ref=col_in.at[yy],
            send_sem=col_send,
            recv_sem=col_recv,
            device_id=(mod(seq + ROW * i, NSEQ), chan),
            device_id_type=MESH,
        ).start()

    for h in range(FILTERS, HEADS):
        filters(h)

    @pl.when(seq > 0)
    def _():
        rim(2).wait_recv()

    @pl.loop(0, QUERIES)
    def _(i):
        query(i)

    pltpu.make_async_copy(three, three, col_recv).wait()
    before = jnp.zeros((MODES, WIDE), F32)
    for y in range(NSEQ // ROW - 1):
        before = jnp.where(y < yy, whole * before + col_in[y], before)
    for r in range(ROW):
        state_out[r] = before
        before = shard * before + row_in[r]
    state[rr] = state_out[rr]

    for i in range(1, ROW):
        r = mod(rr + i, ROW)
        pltpu.make_async_remote_copy(
            src_ref=state_out.at[r],
            dst_ref=state.at[rr],
            send_sem=state_send,
            recv_sem=state_recv,
            device_id=(yy * ROW + r, chan),
            device_id_type=MESH,
        ).start()

    @pl.loop(QUERIES, MORE)
    def _(i):
        query(i)

    pltpu.make_async_copy(seven, seven, state_recv).wait()

    def mix(i):
        @pl.when(i >= MORE)
        def _():
            query(i)

        h = group_of(i)
        step = jnp.exp(decays[h] * -float(BLOCK))
        here = state[h]
        for block in range(BLOCKS):
            rows = pl.ds(block * BLOCK, BLOCK)
            g = gated[h, rows, :]
            high, low = split(here)
            rest = jnp.zeros((BLOCK - 3 * MODES, WIDE), BF16)
            stacked = jnp.concatenate([high, high, low, rest], axis=0)
            conv = matmul(toeplitz[h], jnp.concatenate([g, g], axis=0))
            conv = conv + matmul(from_state[h], stacked)
            m = q_mix[h, rows, :].astype(F32) * conv
            mixed[h, :, rows] = m.T.astype(BF16)
            if block < BLOCKS - 1:
                here = step * here + part[h, block]

    def send(i, a, b):
        h = group_of(i)
        sub = 2 * mod(side + a, 2) + mod(core + b, 2)
        j = (WIDE // SUB) * h + sub
        source = mixed.at[h, pl.ds(pl.multiple_of(sub * SUB, SUB), SUB), :]

        @pl.when(j == seq)
        def _():
            pltpu.make_async_copy(source, middle.at[seq], a_recv.at[seq]).start()

        @pl.when(j != seq)
        def _():
            pltpu.make_async_remote_copy(
                src_ref=source,
                dst_ref=middle.at[seq],
                send_sem=a_send,
                recv_sem=a_recv.at[seq],
                device_id=(j, chan),
                device_id_type=MESH,
            ).start()

    def forward(i, a, b):
        source = source_of(i, a, b)
        plane = source // 4
        tokens = pl.multiple_of(mod(source, 4) * ROWS, ROWS)
        place = out_ref.at[chan, :, pl.ds(tokens, ROWS)]
        block = middle.at[source]
        pltpu.make_async_copy(block, block, a_recv.at[source]).wait()

        @pl.when(plane == chan)
        def _():
            pltpu.make_async_copy(block, place, b_recv).start()

        @pl.when(plane != chan)
        def _():
            pltpu.make_async_remote_copy(
                src_ref=block,
                dst_ref=place,
                send_sem=b_send,
                recv_sem=b_recv,
                device_id=(seq, plane),
                device_id_type=MESH,
            ).start()

    def in_order(turn, m):
        turn(m // 4, mod(m // 2, 2), mod(m, 2))

    @pl.loop(0, NSEQ + AHEAD)
    def _(m):
        @pl.when(jnp.logical_and(m < NSEQ, mod(m, 4) == 0))
        def _():
            mix(m // 4)

        @pl.when(m < NSEQ)
        def _():
            in_order(send, m)

        @pl.when(m >= AHEAD)
        def _():
            in_order(forward, m - AHEAD)

    @pl.when(seq < NSEQ - 1)
    def _():
        for n in range(3):
            rim(n).wait_send()

    pltpu.make_async_copy(seven, seven, local_send).wait()
    pltpu.make_async_copy(three, three, col_send).wait()
    pltpu.make_async_copy(seven, seven, state_send).wait()
    sent = middle.at[pl.ds(0, NSEQ - 1)]
    pltpu.make_async_copy(sent, sent, a_send).wait()
    sent = middle.at[pl.ds(0, NSEQ - NSEQ // NCHAN)]
    pltpu.make_async_copy(sent, sent, b_send).wait()
    pltpu.make_async_copy(out_ref, out_ref, b_recv).wait()


def per_device(q_proj, k_proj, v_proj, short_filter, decay_rate, residue):
    dma = pltpu.SemaphoreType.DMA
    beside = ((0, 0), (0, 0), (0, HEADS * WIDE - MODES))
    params = jnp.concatenate(
        [
            jnp.pad(short_filter, ((0, 0), (0, HEADS - 3), (0, 0))),
            jnp.pad(decay_rate[None], beside),
            jnp.pad(residue[None], beside),
        ]
    )
    raw = pltpu.VMEM((PAD + ROWS, HEADS * WIDE), BF16)
    out = pl.pallas_call(
        kernel,
        out_shape=jax.ShapeDtypeStruct((NCHAN, SUB, 4 * ROWS), BF16),
        in_specs=[pl.BlockSpec(memory_space=pl.ANY)] * 3 + [pl.BlockSpec(memory_space=pltpu.VMEM)],
        out_specs=pl.BlockSpec(memory_space=pl.ANY),
        scratch_shapes=[
            raw, raw, raw,
            pltpu.VMEM((HEADS, ROWS, WIDE), BF16),
            pltpu.VMEM((HEADS, ROWS, WIDE), BF16),
            pltpu.VMEM((HEADS, BLOCK, 2 * BLOCK), BF16),
            pltpu.VMEM((HEADS, BLOCK, BLOCK), BF16),
            pltpu.VMEM((HEADS, 2 * MODES, BLOCK), BF16),
            pltpu.VMEM((HEADS, MODES, WIDE), F32),
            pltpu.VMEM((HEADS, 2, MODES, WIDE), F32),
            pltpu.VMEM((HEADS, BLOCKS, MODES, WIDE), F32),
            pltpu.VMEM((HEADS, MODES, WIDE), F32),
            pltpu.VMEM((ROW, MODES, WIDE), F32),
            pltpu.VMEM((NSEQ // ROW, MODES, WIDE), F32),
            pltpu.VMEM((MODES, WIDE), F32),
            pltpu.VMEM((ROW, MODES, WIDE), F32),
            pltpu.VMEM((HEADS, MODES, WIDE), F32),
            pltpu.VMEM((HEADS, WIDE, ROWS), BF16),
            pltpu.VMEM((NSEQ, SUB, ROWS), BF16),
            dma((1,)), dma((LOADS,)), dma((LOADS,)),
            dma((3,)), dma((3,)),
            dma, dma, dma, dma, dma, dma,
            dma, dma((NSEQ,)), dma, dma,
        ],
        compiler_params=pltpu.CompilerParams(
            collective_id=0, has_side_effects=True, vmem_limit_bytes=50 << 20
        ),
        name="hyena",
    )(q_proj, k_proj, v_proj, params)
    return out[None]


def solution(mesh):
    in_specs = (
        P("seq", "chan"),
        P("seq", "chan"),
        P("seq", "chan"),
        P(None, None, "chan"),
        P("chan", None),
        P("chan", None),
    )
    out_specs = P("seq", None, None, "chan")
    return jax.shard_map(
        per_device, mesh=mesh, in_specs=in_specs, out_specs=out_specs, check_vma=False
    )
```

```python
import functools

import jax
import jax.numpy as jnp
from jax import lax
from jax.experimental import pallas as pl
from jax.experimental.pallas import tpu as pltpu
from jax.sharding import PartitionSpec as P

MESH = pl.DeviceIdType.MESH
F32, BF16 = jnp.float32, jnp.bfloat16

ROWS = 1024
HEADS = 8
WIDE = 128
MODES = 16
BLOCK = 128
BLOCKS = ROWS // BLOCK
PAD = 16
NSEQ = 32
NCHAN = 8
SUB = 32
ROW = 8
LOADS = 4
FILTERS = 1
QUERIES = 2
MORE = 5
AHEAD = 4


def split(x):
    high = x.astype(BF16)
    return high, (x - high.astype(F32)).astype(BF16)


def matmul(a, b):
    return jnp.dot(a, b, preferred_element_type=F32)


def mod(a, b):
    return lax.rem(a, b)


def kernel(
    q_ref, k_ref, v_ref, params_ref, out_ref,
    q_raw, k_raw, v_raw, gated, q_mix, toeplitz, from_state, into_state,
    decays, first_on, part, local, row_in, col_in, col_out, state_out, state, mixed, middle,
    load_q, load_k, load_v, rim_send, rim_recv,
    local_send, row_recv, col_send, col_recv, state_send, state_recv,
    a_send, a_recv, b_send, b_recv,
):
    seq, chan = lax.axis_index("seq"), lax.axis_index("chan")
    yy, rr = seq // ROW, mod(seq, ROW)

    def columns_of(h):
        return pl.ds(pl.multiple_of(h * WIDE, WIDE), WIDE)

    def load(ref, raw, sem, n, parts):
        width = HEADS * WIDE // parts
        columns = pl.ds(pl.multiple_of(n * width, width), width)
        return pltpu.make_async_copy(
            ref.at[:, columns], raw.at[pl.ds(PAD, ROWS), columns], sem.at[n]
        )

    load(k_ref, k_raw, load_k, 0, LOADS).start()
    load(v_ref, v_raw, load_v, 0, LOADS).start()

    barrier = pltpu.get_barrier_semaphore()

    def here_for(to_seq, to_chan):
        pl.semaphore_signal(barrier, inc=1, device_id=(to_seq, to_chan), device_id_type=MESH)

    for i in range(1, NCHAN):
        here_for(seq, mod(chan + i, NCHAN))
    for i in range(1, ROW):
        here_for(yy * ROW + mod(rr + i, ROW), chan)

    @pl.when(jnp.logical_and(rr == 0, yy > 0))
    def _():
        here_for(seq - 1, chan)

    for i in range(1, NSEQ // ROW):
        here_for(mod(seq + i * ROW, NSEQ), chan)

    for n in range(1, LOADS):
        load(k_ref, k_raw, load_k, n, LOADS).start()
        load(v_ref, v_raw, load_v, n, LOADS).start()
    load(q_ref, q_raw, load_q, 0, 1).start()

    ones_at = lax.broadcasted_iota(jnp.int32, (MODES, MODES), 0) == lax.broadcasted_iota(
        jnp.int32, (MODES, MODES), 1
    )
    lane = lax.broadcasted_iota(jnp.int32, (MODES, BLOCK), 1)
    causal = lax.broadcasted_iota(jnp.int32, (BLOCK, BLOCK), 0) >= lax.broadcasted_iota(
        jnp.int32, (BLOCK, BLOCK), 1
    )

    def column(row):
        wide = jnp.where(ones_at, jnp.broadcast_to(row, (MODES, MODES)), 0.0)
        return jnp.broadcast_to(jnp.sum(wide, axis=1, keepdims=True), (MODES, WIDE))

    for h in range(HEADS):
        rate = column(params_ref[3, h : h + 1, 0:MODES])
        decays[h] = rate
        first_on[h, 0] = jnp.exp(rate * -float(ROWS - 1))
        first_on[h, 1] = jnp.exp(rate * -float(ROWS - 2))
        high, low = split(jnp.exp(-rate * (BLOCK - 1 - lane).astype(F32)))
        into_state[h, 0:MODES] = high
        into_state[h, MODES : 2 * MODES] = low

    def filters(h):
        rate = decays[h]
        weight = column(params_ref[4, h : h + 1, 0:MODES])
        lag = jnp.where(lane == 0, 0, BLOCK - lane).astype(F32)
        first = jnp.sum(weight * jnp.exp(-rate * lag), axis=0, keepdims=True)
        turned = pltpu.roll(
            jnp.broadcast_to(first, (BLOCK, BLOCK)), 0, 1, stride=1, stride_axis=0
        )
        high, low = split(jnp.where(causal, turned, 0.0))
        toeplitz[h, :, 0:BLOCK] = high
        toeplitz[h, :, BLOCK : 2 * BLOCK] = low
        high, low = split(weight * jnp.exp(-rate * (lane + 1).astype(F32)))
        high, low = high.astype(F32), low.astype(F32)
        rest = jnp.zeros((BLOCK - 3 * MODES, BLOCK), F32)
        from_state[h] = jnp.concatenate([high, low, high, rest], axis=0).T.astype(BF16)

    def taps_of(raw, branch, h, start, count):
        columns = columns_of(h)
        x = raw[pl.ds(start, count), columns].astype(F32)
        y = params_ref[branch, 0:1, columns] * x
        y = y + params_ref[branch, 1:2, columns] * pltpu.roll(x, 1, 0)
        return y + params_ref[branch, 2:3, columns] * pltpu.roll(x, 2, 0)

    def short(raw, branch, h, row, count):
        return taps_of(raw, branch, h, row, count + PAD)[PAD:]

    inner = lax.broadcasted_iota(jnp.int32, (BLOCK, WIDE), 0) >= 2

    def gate(h, block):
        row = block * BLOCK
        if block:
            g = short(k_raw, 1, h, row, BLOCK) * short(v_raw, 2, h, row, BLOCK)
        else:
            g = taps_of(k_raw, 1, h, PAD, BLOCK) * taps_of(v_raw, 2, h, PAD, BLOCK)
            g = jnp.where(inner, g, 0.0)
        g = g.astype(BF16)
        gated[h, pl.ds(row, BLOCK), :] = g
        both = matmul(into_state[h], g)
        both = both[0:MODES] + both[MODES : 2 * MODES]
        part[h, block] = both
        return both

    def loaded(n):
        load(k_ref, k_raw, load_k, n, LOADS).wait()
        load(v_ref, v_raw, load_v, n, LOADS).wait()

    def gates(n):
        for k in range(HEADS // LOADS):
            h = n * (HEADS // LOADS) + k
            step = jnp.exp(decays[h] * -float(BLOCK))
            total = gate(h, 0)
            for block in range(1, BLOCKS):
                total = step * total + gate(h, block)
            local[h] = total

    loaded(0)
    gates(0)
    for n in range(1, LOADS):
        loaded(n)

    ends_row = jnp.logical_and(rr == ROW - 1, yy < NSEQ // ROW - 1)
    greeted = ROW - 1 + NSEQ // ROW - 1 + NCHAN - 1

    @pl.when(ends_row)
    def _():
        pl.semaphore_wait(barrier, greeted + 1)

    @pl.when(jnp.logical_not(ends_row))
    def _():
        pl.semaphore_wait(barrier, greeted)

    def rim(n):
        raw = (k_raw, v_raw, q_raw)[n]
        return pltpu.make_async_remote_copy(
            src_ref=raw.at[pl.ds(ROWS, PAD), :],
            dst_ref=raw.at[pl.ds(0, PAD), :],
            send_sem=rim_send.at[n],
            recv_sem=rim_recv.at[n],
            device_id=(mod(seq + 1, NSEQ), chan),
            device_id_type=MESH,
        )

    @pl.when(seq < NSEQ - 1)
    def _():
        for n in range(2):
            rim(n).start()

    @pl.when(seq == 0)
    def _():
        for raw in (k_raw, v_raw, q_raw):
            raw[0:PAD, :] = jnp.zeros((PAD, HEADS * WIDE), BF16)

    for n in range(1, LOADS):
        gates(n)

    @pl.when(seq > 0)
    def _():
        for n in range(2):
            rim(n).wait_recv()

    firsts = []
    for h in range(HEADS):
        g = taps_of(k_raw, 1, h, 0, 2 * PAD) * taps_of(v_raw, 2, h, 0, 2 * PAD)
        g = g[PAD:].astype(BF16)
        gated[h, 0:PAD, :] = g
        g = g.astype(F32)[0:2]
        firsts.append(g)
        local[h] = local[h] + first_on[h, 0] * g[0:1] + first_on[h, 1] * g[1:2]
    row_in[rr] = local[rr]

    for i in range(1, ROW):
        h = mod(rr + i, ROW)
        pltpu.make_async_remote_copy(
            src_ref=local.at[h],
            dst_ref=row_in.at[rr],
            send_sem=local_send,
            recv_sem=row_recv,
            device_id=(yy * ROW + h, chan),
            device_id_type=MESH,
        ).start()

    load(q_ref, q_raw, load_q, 0, 1).wait()

    @pl.when(seq < NSEQ - 1)
    def _():
        rim(2).start()

    for h in range(HEADS):
        g, rate = firsts[h], decays[h]
        part[h, 0] = (
            part[h, 0]
            + jnp.exp(rate * -float(BLOCK - 1)) * g[0:1]
            + jnp.exp(rate * -float(BLOCK - 2)) * g[1:2]
        )

    side, core, half = mod(rr // 2, 2), mod(rr, 2), rr // 4
    parity = mod(half + chan, 2)
    base = 2 * (1 - side + 2 * core) + parity + 2 * yy - 2 * ((chan + parity) // 2) + 2 * NCHAN

    def group_of(i):
        return mod(base + i, HEADS)

    def source_of(i, a, b):
        odd = mod(seq // 4 - i + HEADS, 2)
        turn = mod(seq // 4 - i - odd + HEADS, HEADS) // 2
        s, c = mod(side + a, 2), mod(core + b, 2)
        y = mod(turn - (1 - s) - 2 * c + (chan + odd) // 2 + NSEQ // ROW, NSEQ // ROW)
        return ROW * y + 4 * mod(odd + chan, 2) + 2 * s + c

    def query(i):
        h = group_of(i)
        for block in range(BLOCKS):
            row = block * BLOCK
            q_mix[h, pl.ds(row, BLOCK), :] = short(q_raw, 0, h, row, BLOCK).astype(BF16)

    for h in range(FILTERS):
        filters(h)

    seven = row_in.at[pl.ds(0, ROW - 1)]
    three = col_in.at[pl.ds(0, NSEQ // ROW - 1)]
    pltpu.make_async_copy(seven, seven, row_recv).wait()
    rate = decays[rr]
    shard = jnp.exp(rate * -float(ROWS))
    whole = jnp.exp(rate * -float(ROWS * ROW))
    total = row_in[0]
    for r in range(1, ROW):
        total = shard * total + row_in[r]
    col_out[...] = total
    col_in[yy] = total

    for i in range(1, NSEQ // ROW):
        pltpu.make_async_remote_copy(
            src_ref=col_out,
            dst_ref=col_in.at[yy],
            send_sem=col_send,
            recv_sem=col_recv,
            device_id=(mod(seq + ROW * i, NSEQ), chan),
            device_id_type=MESH,
        ).start()

    for h in range(FILTERS, HEADS):
        filters(h)

    @pl.when(seq > 0)
    def _():
        rim(2).wait_recv()

    @pl.loop(0, QUERIES)
    def _(i):
        query(i)

    pltpu.make_async_copy(three, three, col_recv).wait()
    before = jnp.zeros((MODES, WIDE), F32)
    for y in range(NSEQ // ROW - 1):
        before = jnp.where(y < yy, whole * before + col_in[y], before)
    for r in range(ROW):
        state_out[r] = before
        before = shard * before + row_in[r]
    state[rr] = state_out[rr]

    for i in range(1, ROW):
        r = mod(rr + i, ROW)
        pltpu.make_async_remote_copy(
            src_ref=state_out.at[r],
            dst_ref=state.at[rr],
            send_sem=state_send,
            recv_sem=state_recv,
            device_id=(yy * ROW + r, chan),
            device_id_type=MESH,
        ).start()

    @pl.loop(QUERIES, MORE)
    def _(i):
        query(i)

    pltpu.make_async_copy(seven, seven, state_recv).wait()

    def mix(i):
        @pl.when(i >= MORE)
        def _():
            query(i)

        h = group_of(i)
        step = jnp.exp(decays[h] * -float(BLOCK))
        here = state[h]
        for block in range(BLOCKS):
            rows = pl.ds(block * BLOCK, BLOCK)
            g = gated[h, rows, :]
            high, low = split(here)
            rest = jnp.zeros((BLOCK - 3 * MODES, WIDE), BF16)
            stacked = jnp.concatenate([high, high, low, rest], axis=0)
            conv = matmul(toeplitz[h], jnp.concatenate([g, g], axis=0))
            conv = conv + matmul(from_state[h], stacked)
            m = q_mix[h, rows, :].astype(F32) * conv
            mixed[h, :, rows] = m.T.astype(BF16)
            if block < BLOCKS - 1:
                here = step * here + part[h, block]

    def send(i, a, b):
        h = group_of(i)
        sub = 2 * mod(side + a, 2) + mod(core + b, 2)
        j = (WIDE // SUB) * h + sub
        source = mixed.at[h, pl.ds(pl.multiple_of(sub * SUB, SUB), SUB), :]

        @pl.when(j == seq)
        def _():
            pltpu.make_async_copy(source, middle.at[seq], a_recv.at[seq]).start()

        @pl.when(j != seq)
        def _():
            pltpu.make_async_remote_copy(
                src_ref=source,
                dst_ref=middle.at[seq],
                send_sem=a_send,
                recv_sem=a_recv.at[seq],
                device_id=(j, chan),
                device_id_type=MESH,
            ).start()

    def forward(i, a, b):
        source = source_of(i, a, b)
        plane = source // 4
        tokens = pl.multiple_of(mod(source, 4) * ROWS, ROWS)
        place = out_ref.at[chan, :, pl.ds(tokens, ROWS)]
        block = middle.at[source]
        pltpu.make_async_copy(block, block, a_recv.at[source]).wait()

        @pl.when(plane == chan)
        def _():
            pltpu.make_async_copy(block, place, b_recv).start()

        @pl.when(plane != chan)
        def _():
            pltpu.make_async_remote_copy(
                src_ref=block,
                dst_ref=place,
                send_sem=b_send,
                recv_sem=b_recv,
                device_id=(seq, plane),
                device_id_type=MESH,
            ).start()

    def in_order(turn, m):
        turn(m // 4, mod(m // 2, 2), mod(m, 2))

    @pl.loop(0, NSEQ + AHEAD)
    def _(m):
        @pl.when(jnp.logical_and(m < NSEQ, mod(m, 4) == 0))
        def _():
            mix(m // 4)

        @pl.when(m < NSEQ)
        def _():
            in_order(send, m)

        @pl.when(m >= AHEAD)
        def _():
            in_order(forward, m - AHEAD)

    @pl.when(seq < NSEQ - 1)
    def _():
        for n in range(3):
            rim(n).wait_send()

    pltpu.make_async_copy(seven, seven, local_send).wait()
    pltpu.make_async_copy(three, three, col_send).wait()
    pltpu.make_async_copy(seven, seven, state_send).wait()
    sent = middle.at[pl.ds(0, NSEQ - 1)]
    pltpu.make_async_copy(sent, sent, a_send).wait()
    sent = middle.at[pl.ds(0, NSEQ - NSEQ // NCHAN)]
    pltpu.make_async_copy(sent, sent, b_send).wait()
    pltpu.make_async_copy(out_ref, out_ref, b_recv).wait()


def per_device(q_proj, k_proj, v_proj, short_filter, decay_rate, residue):
    dma = pltpu.SemaphoreType.DMA
    beside = ((0, 0), (0, 0), (0, HEADS * WIDE - MODES))
    params = jnp.concatenate(
        [
            jnp.pad(short_filter, ((0, 0), (0, HEADS - 3), (0, 0))),
            jnp.pad(decay_rate[None], beside),
            jnp.pad(residue[None], beside),
        ]
    )
    raw = pltpu.VMEM((PAD + ROWS, HEADS * WIDE), BF16)
    out = pl.pallas_call(
        kernel,
        out_shape=jax.ShapeDtypeStruct((NCHAN, SUB, 4 * ROWS), BF16),
        in_specs=[pl.BlockSpec(memory_space=pl.ANY)] * 3 + [pl.BlockSpec(memory_space=pltpu.VMEM)],
        out_specs=pl.BlockSpec(memory_space=pl.ANY),
        scratch_shapes=[
            raw, raw, raw,
            pltpu.VMEM((HEADS, ROWS, WIDE), BF16),
            pltpu.VMEM((HEADS, ROWS, WIDE), BF16),
            pltpu.VMEM((HEADS, BLOCK, 2 * BLOCK), BF16),
            pltpu.VMEM((HEADS, BLOCK, BLOCK), BF16),
            pltpu.VMEM((HEADS, 2 * MODES, BLOCK), BF16),
            pltpu.VMEM((HEADS, MODES, WIDE), F32),
            pltpu.VMEM((HEADS, 2, MODES, WIDE), F32),
            pltpu.VMEM((HEADS, BLOCKS, MODES, WIDE), F32),
            pltpu.VMEM((HEADS, MODES, WIDE), F32),
            pltpu.VMEM((ROW, MODES, WIDE), F32),
            pltpu.VMEM((NSEQ // ROW, MODES, WIDE), F32),
            pltpu.VMEM((MODES, WIDE), F32),
            pltpu.VMEM((ROW, MODES, WIDE), F32),
            pltpu.VMEM((HEADS, MODES, WIDE), F32),
            pltpu.VMEM((HEADS, WIDE, ROWS), BF16),
            pltpu.VMEM((NSEQ, SUB, ROWS), BF16),
            dma((1,)), dma((LOADS,)), dma((LOADS,)),
            dma((3,)), dma((3,)),
            dma, dma, dma, dma, dma, dma,
            dma, dma((NSEQ,)), dma, dma,
        ],
        compiler_params=pltpu.CompilerParams(
            collective_id=0, has_side_effects=True, vmem_limit_bytes=50 << 20
        ),
        name="hyena",
    )(q_proj, k_proj, v_proj, params)
    return out[None]


def solution(mesh):
    in_specs = (
        P("seq", "chan"),
        P("seq", "chan"),
        P("seq", "chan"),
        P(None, None, "chan"),
        P("chan", None),
        P("chan", None),
    )
    out_specs = P("seq", None, None, "chan")
    return jax.shard_map(
        per_device, mesh=mesh, in_specs=in_specs, out_specs=out_specs, check_vma=False
    )
```

```python
import functools

import jax
import jax.numpy as jnp
from jax import lax
from jax.experimental import pallas as pl
from jax.experimental.pallas import tpu as pltpu
from jax.sharding import PartitionSpec as P

MESH = pl.DeviceIdType.MESH
F32, BF16 = jnp.float32, jnp.bfloat16

ROWS = 1024
HEADS = 8
WIDE = 128
MODES = 16
BLOCK = 128
BLOCKS = ROWS // BLOCK
PAD = 16
NSEQ = 32
NCHAN = 8
SUB = 32
ROW = 8
LOADS = 4
FILTERS = 1
QUERIES = 2
MORE = 5
AHEAD = 4


def split(x):
    high = x.astype(BF16)
    return high, (x - high.astype(F32)).astype(BF16)


def matmul(a, b):
    return jnp.dot(a, b, preferred_element_type=F32)


def mod(a, b):
    return lax.rem(a, b)


def kernel(
    q_ref, k_ref, v_ref, params_ref, out_ref,
    q_raw, k_raw, v_raw, gated, q_mix, toeplitz, from_state, into_state,
    decays, first_on, part, local, row_in, col_in, col_out, state_out, state, mixed, middle,
    load_q, load_k, load_v, rim_send, rim_recv,
    local_send, row_recv, col_send, col_recv, state_send, state_recv,
    a_send, a_recv, b_send, b_recv,
):
    seq, chan = lax.axis_index("seq"), lax.axis_index("chan")
    yy, rr = seq // ROW, mod(seq, ROW)

    def columns_of(h):
        return pl.ds(pl.multiple_of(h * WIDE, WIDE), WIDE)

    def load(ref, raw, sem, n, parts):
        width = HEADS * WIDE // parts
        columns = pl.ds(pl.multiple_of(n * width, width), width)
        return pltpu.make_async_copy(
            ref.at[:, columns], raw.at[pl.ds(PAD, ROWS), columns], sem.at[n]
        )

    load(k_ref, k_raw, load_k, 0, LOADS).start()
    load(v_ref, v_raw, load_v, 0, LOADS).start()

    barrier = pltpu.get_barrier_semaphore()

    def here_for(to_seq, to_chan):
        pl.semaphore_signal(barrier, inc=1, device_id=(to_seq, to_chan), device_id_type=MESH)

    for i in range(1, NCHAN):
        here_for(seq, mod(chan + i, NCHAN))
    for i in range(1, ROW):
        here_for(yy * ROW + mod(rr + i, ROW), chan)

    @pl.when(jnp.logical_and(rr == 0, yy > 0))
    def _():
        here_for(seq - 1, chan)

    for i in range(1, NSEQ // ROW):
        here_for(mod(seq + i * ROW, NSEQ), chan)

    for n in range(1, LOADS):
        load(k_ref, k_raw, load_k, n, LOADS).start()
        load(v_ref, v_raw, load_v, n, LOADS).start()
    load(q_ref, q_raw, load_q, 0, 1).start()

    ones_at = lax.broadcasted_iota(jnp.int32, (MODES, MODES), 0) == lax.broadcasted_iota(
        jnp.int32, (MODES, MODES), 1
    )
    lane = lax.broadcasted_iota(jnp.int32, (MODES, BLOCK), 1)
    causal = lax.broadcasted_iota(jnp.int32, (BLOCK, BLOCK), 0) >= lax.broadcasted_iota(
        jnp.int32, (BLOCK, BLOCK), 1
    )

    def column(row):
        wide = jnp.where(ones_at, jnp.broadcast_to(row, (MODES, MODES)), 0.0)
        return jnp.broadcast_to(jnp.sum(wide, axis=1, keepdims=True), (MODES, WIDE))

    for h in range(HEADS):
        rate = column(params_ref[3, h : h + 1, 0:MODES])
        decays[h] = rate
        first_on[h, 0] = jnp.exp(rate * -float(ROWS - 1))
        first_on[h, 1] = jnp.exp(rate * -float(ROWS - 2))
        high, low = split(jnp.exp(-rate * (BLOCK - 1 - lane).astype(F32)))
        into_state[h, 0:MODES] = high
        into_state[h, MODES : 2 * MODES] = low

    def filters(h):
        rate = decays[h]
        weight = column(params_ref[4, h : h + 1, 0:MODES])
        lag = jnp.where(lane == 0, 0, BLOCK - lane).astype(F32)
        first = jnp.sum(weight * jnp.exp(-rate * lag), axis=0, keepdims=True)
        turned = pltpu.roll(
            jnp.broadcast_to(first, (BLOCK, BLOCK)), 0, 1, stride=1, stride_axis=0
        )
        high, low = split(jnp.where(causal, turned, 0.0))
        toeplitz[h, :, 0:BLOCK] = high
        toeplitz[h, :, BLOCK : 2 * BLOCK] = low
        high, low = split(weight * jnp.exp(-rate * (lane + 1).astype(F32)))
        high, low = high.astype(F32), low.astype(F32)
        rest = jnp.zeros((BLOCK - 3 * MODES, BLOCK), F32)
        from_state[h] = jnp.concatenate([high, low, high, rest], axis=0).T.astype(BF16)

    def taps_of(raw, branch, h, start, count):
        columns = columns_of(h)
        x = raw[pl.ds(start, count), columns].astype(F32)
        y = params_ref[branch, 0:1, columns] * x
        y = y + params_ref[branch, 1:2, columns] * pltpu.roll(x, 1, 0)
        return y + params_ref[branch, 2:3, columns] * pltpu.roll(x, 2, 0)

    def short(raw, branch, h, row, count):
        return taps_of(raw, branch, h, row, count + PAD)[PAD:]

    inner = lax.broadcasted_iota(jnp.int32, (BLOCK, WIDE), 0) >= 2

    def gate(h, block):
        row = block * BLOCK
        if block:
            g = short(k_raw, 1, h, row, BLOCK) * short(v_raw, 2, h, row, BLOCK)
        else:
            g = taps_of(k_raw, 1, h, PAD, BLOCK) * taps_of(v_raw, 2, h, PAD, BLOCK)
            g = jnp.where(inner, g, 0.0)
        g = g.astype(BF16)
        gated[h, pl.ds(row, BLOCK), :] = g
        both = matmul(into_state[h], g)
        both = both[0:MODES] + both[MODES : 2 * MODES]
        part[h, block] = both
        return both

    def loaded(n):
        load(k_ref, k_raw, load_k, n, LOADS).wait()
        load(v_ref, v_raw, load_v, n, LOADS).wait()

    def gates(n):
        for k in range(HEADS // LOADS):
            h = n * (HEADS // LOADS) + k
            step = jnp.exp(decays[h] * -float(BLOCK))
            total = gate(h, 0)
            for block in range(1, BLOCKS):
                total = step * total + gate(h, block)
            local[h] = total

    loaded(0)
    gates(0)
    for n in range(1, LOADS):
        loaded(n)

    ends_row = jnp.logical_and(rr == ROW - 1, yy < NSEQ // ROW - 1)
    greeted = ROW - 1 + NSEQ // ROW - 1 + NCHAN - 1

    @pl.when(ends_row)
    def _():
        pl.semaphore_wait(barrier, greeted + 1)

    @pl.when(jnp.logical_not(ends_row))
    def _():
        pl.semaphore_wait(barrier, greeted)

    def rim(n):
        raw = (k_raw, v_raw, q_raw)[n]
        return pltpu.make_async_remote_copy(
            src_ref=raw.at[pl.ds(ROWS, PAD), :],
            dst_ref=raw.at[pl.ds(0, PAD), :],
            send_sem=rim_send.at[n],
            recv_sem=rim_recv.at[n],
            device_id=(mod(seq + 1, NSEQ), chan),
            device_id_type=MESH,
        )

    @pl.when(seq < NSEQ - 1)
    def _():
        for n in range(2):
            rim(n).start()

    @pl.when(seq == 0)
    def _():
        for raw in (k_raw, v_raw, q_raw):
            raw[0:PAD, :] = jnp.zeros((PAD, HEADS * WIDE), BF16)

    for n in range(1, LOADS):
        gates(n)

    @pl.when(seq > 0)
    def _():
        for n in range(2):
            rim(n).wait_recv()

    firsts = []
    for h in range(HEADS):
        g = taps_of(k_raw, 1, h, 0, 2 * PAD) * taps_of(v_raw, 2, h, 0, 2 * PAD)
        g = g[PAD:].astype(BF16)
        gated[h, 0:PAD, :] = g
        g = g.astype(F32)[0:2]
        firsts.append(g)
        total = local[h] + first_on[h, 0] * g[0:1] + first_on[h, 1] * g[1:2]
        local[h] = total

        @pl.when(h == rr)
        def _():
            row_in[rr] = total

        @pl.when(h != rr)
        def _():
            pltpu.make_async_remote_copy(
                src_ref=local.at[h],
                dst_ref=row_in.at[rr],
                send_sem=local_send,
                recv_sem=row_recv,
                device_id=(yy * ROW + h, chan),
                device_id_type=MESH,
            ).start()

    load(q_ref, q_raw, load_q, 0, 1).wait()

    @pl.when(seq < NSEQ - 1)
    def _():
        rim(2).start()

    for h in range(HEADS):
        g, rate = firsts[h], decays[h]
        part[h, 0] = (
            part[h, 0]
            + jnp.exp(rate * -float(BLOCK - 1)) * g[0:1]
            + jnp.exp(rate * -float(BLOCK - 2)) * g[1:2]
        )

    side, core, half = mod(rr // 2, 2), mod(rr, 2), rr // 4
    parity = mod(half + chan, 2)
    base = 2 * (1 - side + 2 * core) + parity + 2 * yy - 2 * ((chan + parity) // 2) + 2 * NCHAN

    def group_of(i):
        return mod(base + i, HEADS)

    def source_of(i, a, b):
        odd = mod(seq // 4 - i + HEADS, 2)
        turn = mod(seq // 4 - i - odd + HEADS, HEADS) // 2
        s, c = mod(side + a, 2), mod(core + b, 2)
        y = mod(turn - (1 - s) - 2 * c + (chan + odd) // 2 + NSEQ // ROW, NSEQ // ROW)
        return ROW * y + 4 * mod(odd + chan, 2) + 2 * s + c

    def query(i):
        h = group_of(i)
        for block in range(BLOCKS):
            row = block * BLOCK
            q_mix[h, pl.ds(row, BLOCK), :] = short(q_raw, 0, h, row, BLOCK).astype(BF16)

    for h in range(FILTERS):
        filters(h)

    seven = row_in.at[pl.ds(0, ROW - 1)]
    three = col_in.at[pl.ds(0, NSEQ // ROW - 1)]
    pltpu.make_async_copy(seven, seven, row_recv).wait()
    rate = decays[rr]
    shard = jnp.exp(rate * -float(ROWS))
    whole = jnp.exp(rate * -float(ROWS * ROW))
    total = row_in[0]
    for r in range(1, ROW):
        total = shard * total + row_in[r]
    col_out[...] = total
    col_in[yy] = total

    for i in range(1, NSEQ // ROW):
        pltpu.make_async_remote_copy(
            src_ref=col_out,
            dst_ref=col_in.at[yy],
            send_sem=col_send,
            recv_sem=col_recv,
            device_id=(mod(seq + ROW * i, NSEQ), chan),
            device_id_type=MESH,
        ).start()

    for h in range(FILTERS, HEADS):
        filters(h)

    @pl.when(seq > 0)
    def _():
        rim(2).wait_recv()

    @pl.loop(0, QUERIES)
    def _(i):
        query(i)

    pltpu.make_async_copy(three, three, col_recv).wait()
    before = jnp.zeros((MODES, WIDE), F32)
    for y in range(NSEQ // ROW - 1):
        before = jnp.where(y < yy, whole * before + col_in[y], before)
    for r in range(ROW):
        state_out[r] = before

        @pl.when(r == rr)
        def _():
            state[rr] = before

        @pl.when(r != rr)
        def _():
            pltpu.make_async_remote_copy(
                src_ref=state_out.at[r],
                dst_ref=state.at[rr],
                send_sem=state_send,
                recv_sem=state_recv,
                device_id=(yy * ROW + r, chan),
                device_id_type=MESH,
            ).start()

        before = shard * before + row_in[r]

    @pl.loop(QUERIES, MORE)
    def _(i):
        query(i)

    pltpu.make_async_copy(seven, seven, state_recv).wait()

    def mix(i):
        @pl.when(i >= MORE)
        def _():
            query(i)

        h = group_of(i)
        step = jnp.exp(decays[h] * -float(BLOCK))
        here = state[h]
        for block in range(BLOCKS):
            rows = pl.ds(block * BLOCK, BLOCK)
            g = gated[h, rows, :]
            high, low = split(here)
            rest = jnp.zeros((BLOCK - 3 * MODES, WIDE), BF16)
            stacked = jnp.concatenate([high, high, low, rest], axis=0)
            conv = matmul(toeplitz[h], jnp.concatenate([g, g], axis=0))
            conv = conv + matmul(from_state[h], stacked)
            m = q_mix[h, rows, :].astype(F32) * conv
            mixed[h, :, rows] = m.T.astype(BF16)
            if block < BLOCKS - 1:
                here = step * here + part[h, block]

    def send(i, a, b):
        h = group_of(i)
        sub = 2 * mod(side + a, 2) + mod(core + b, 2)
        j = (WIDE // SUB) * h + sub
        source = mixed.at[h, pl.ds(pl.multiple_of(sub * SUB, SUB), SUB), :]

        @pl.when(j == seq)
        def _():
            pltpu.make_async_copy(source, middle.at[seq], a_recv.at[seq]).start()

        @pl.when(j != seq)
        def _():
            pltpu.make_async_remote_copy(
                src_ref=source,
                dst_ref=middle.at[seq],
                send_sem=a_send,
                recv_sem=a_recv.at[seq],
                device_id=(j, chan),
                device_id_type=MESH,
            ).start()

    def forward(i, a, b):
        source = source_of(i, a, b)
        plane = source // 4
        tokens = pl.multiple_of(mod(source, 4) * ROWS, ROWS)
        place = out_ref.at[chan, :, pl.ds(tokens, ROWS)]
        block = middle.at[source]
        pltpu.make_async_copy(block, block, a_recv.at[source]).wait()

        @pl.when(plane == chan)
        def _():
            pltpu.make_async_copy(block, place, b_recv).start()

        @pl.when(plane != chan)
        def _():
            pltpu.make_async_remote_copy(
                src_ref=block,
                dst_ref=place,
                send_sem=b_send,
                recv_sem=b_recv,
                device_id=(seq, plane),
                device_id_type=MESH,
            ).start()

    def in_order(turn, m):
        turn(m // 4, mod(m // 2, 2), mod(m, 2))

    @pl.loop(0, NSEQ + AHEAD)
    def _(m):
        @pl.when(jnp.logical_and(m < NSEQ, mod(m, 4) == 0))
        def _():
            mix(m // 4)

        @pl.when(m < NSEQ)
        def _():
            in_order(send, m)

        @pl.when(m >= AHEAD)
        def _():
            in_order(forward, m - AHEAD)

    @pl.when(seq < NSEQ - 1)
    def _():
        for n in range(3):
            rim(n).wait_send()

    pltpu.make_async_copy(seven, seven, local_send).wait()
    pltpu.make_async_copy(three, three, col_send).wait()
    pltpu.make_async_copy(seven, seven, state_send).wait()
    sent = middle.at[pl.ds(0, NSEQ - 1)]
    pltpu.make_async_copy(sent, sent, a_send).wait()
    sent = middle.at[pl.ds(0, NSEQ - NSEQ // NCHAN)]
    pltpu.make_async_copy(sent, sent, b_send).wait()
    pltpu.make_async_copy(out_ref, out_ref, b_recv).wait()


def per_device(q_proj, k_proj, v_proj, short_filter, decay_rate, residue):
    dma = pltpu.SemaphoreType.DMA
    beside = ((0, 0), (0, 0), (0, HEADS * WIDE - MODES))
    params = jnp.concatenate(
        [
            jnp.pad(short_filter, ((0, 0), (0, HEADS - 3), (0, 0))),
            jnp.pad(decay_rate[None], beside),
            jnp.pad(residue[None], beside),
        ]
    )
    raw = pltpu.VMEM((PAD + ROWS, HEADS * WIDE), BF16)
    out = pl.pallas_call(
        kernel,
        out_shape=jax.ShapeDtypeStruct((NCHAN, SUB, 4 * ROWS), BF16),
        in_specs=[pl.BlockSpec(memory_space=pl.ANY)] * 3 + [pl.BlockSpec(memory_space=pltpu.VMEM)],
        out_specs=pl.BlockSpec(memory_space=pl.ANY),
        scratch_shapes=[
            raw, raw, raw,
            pltpu.VMEM((HEADS, ROWS, WIDE), BF16),
            pltpu.VMEM((HEADS, ROWS, WIDE), BF16),
            pltpu.VMEM((HEADS, BLOCK, 2 * BLOCK), BF16),
            pltpu.VMEM((HEADS, BLOCK, BLOCK), BF16),
            pltpu.VMEM((HEADS, 2 * MODES, BLOCK), BF16),
            pltpu.VMEM((HEADS, MODES, WIDE), F32),
            pltpu.VMEM((HEADS, 2, MODES, WIDE), F32),
            pltpu.VMEM((HEADS, BLOCKS, MODES, WIDE), F32),
            pltpu.VMEM((HEADS, MODES, WIDE), F32),
            pltpu.VMEM((ROW, MODES, WIDE), F32),
            pltpu.VMEM((NSEQ // ROW, MODES, WIDE), F32),
            pltpu.VMEM((MODES, WIDE), F32),
            pltpu.VMEM((ROW, MODES, WIDE), F32),
            pltpu.VMEM((HEADS, MODES, WIDE), F32),
            pltpu.VMEM((HEADS, WIDE, ROWS), BF16),
            pltpu.VMEM((NSEQ, SUB, ROWS), BF16),
            dma((1,)), dma((LOADS,)), dma((LOADS,)),
            dma((3,)), dma((3,)),
            dma, dma, dma, dma, dma, dma,
            dma, dma((NSEQ,)), dma, dma,
        ],
        compiler_params=pltpu.CompilerParams(
            collective_id=0, has_side_effects=True, vmem_limit_bytes=50 << 20
        ),
        name="hyena",
    )(q_proj, k_proj, v_proj, params)
    return out[None]


def solution(mesh):
    in_specs = (
        P("seq", "chan"),
        P("seq", "chan"),
        P("seq", "chan"),
        P(None, None, "chan"),
        P("chan", None),
        P("chan", None),
    )
    out_specs = P("seq", None, None, "chan")
    return jax.shard_map(
        per_device, mesh=mesh, in_specs=in_specs, out_specs=out_specs, check_vma=False
    )
```
